32 devices in a mesh: row: 4 (over z), ma: 8 (over y, x, core).
Axes of the slice: x: 2, y: 2, z: 4, core: 2. Of those that a mesh axis runs over, the one named last changes fastest.
Arguments:
- spectra: float32 [4, 2, 128, 4224], P(None, None, 'row', 'ma'), may hold values from -6 to 6
- dtheta_table: bfloat16 [4224, 768], P('ma'), may hold values from -0.046875 to 0.046875
- dphi_table: bfloat16 [4224, 768], P('ma'), may hold values from -0.046875 to 0.046875
- analysis_table: bfloat16 [4224, 768], P('ma'), may hold values from -6 to 6
- pair_index: int32 [8], replicated, may hold values from 0 to 255, as said below
- diffusivity: float32 [4], replicated, may hold values from 0.0001 to 0.0004
Outputs:
- new_spectra: float32 [4, 2, 128, 4224], P(None, None, 'row', 'ma')
The draws below stay inside these ranges and needn't reach their ends.
Inputs may be any that keep to these rules, and one draw needn't show every extreme that they name: 8 distinct values, among them always both 0 and the largest; position g holds the orders pair_index[g] and 511 - pair_index[g].
All inputs are finite; a program needn't handle non-finite values.
Results may differ from the reference program's by a relative error of at most 0.0057.
Values may be sent and summed in bfloat16 or wider, within the bound.
A program may use at most 64 MiB of HBM per device.

```python
import math
import jax
import jax.numpy as jnp
from jax import lax

LMAX = 511
NTH = 768
NPHI = 1536
SLOTS = 528
NR = 128
NPAIRS = 8


def draw_pair_index(key, part):
    half_count = (LMAX + 1) // 2
    first_key, second_key = jax.random.split(key)
    middle = jax.random.permutation(first_key, half_count - 2)[:NPAIRS - 2].astype(jnp.int32) + 1
    ends = jnp.array([0, half_count - 1], dtype=jnp.int32)
    values = jnp.concatenate([ends, middle])
    return jax.random.permutation(second_key, values).astype(jnp.int32)


def level_of(own_key, extent, cuts, least, largest):
    gain = 1.0
    for axis_at, parts in cuts:
        heights = jax.random.uniform(jax.random.fold_in(jax.random.fold_in(own_key, 6), axis_at), (parts,), jnp.float32, least / len(cuts), largest / len(cuts))
        gain = gain * jnp.repeat(jnp.exp(heights), extent[axis_at] // parts).reshape((-1,) + (1,) * (len(extent) - 1 - axis_at))
    return gain


def centred(rng, dims, deviation, bound, cuts=(), held_as=jnp.bfloat16):
    loudness = level_of(rng, dims, cuts, -0.22, 0.18) if cuts else 1.0
    drawn = jax.random.normal(rng, dims, jnp.float32) * deviation * loudness
    return jnp.minimum(jnp.maximum(drawn, -bound), bound).astype(held_as)


def setup_inputs(seed: int = 0) -> dict:
    arg_keys = jax.random.split(jax.random.key(seed), 7)
    return {
        "spectra": centred(arg_keys[0], (4, 2, NR, NPAIRS * SLOTS), 1.0, 6.0, ((2, 4), (3, 8)), jnp.float32),
        "dtheta_table": centred(arg_keys[1], (NPAIRS * SLOTS, NTH), (4 * NPAIRS * (LMAX + 1)) ** -0.5, 0.046875, ((0, 8),)),
        "dphi_table": centred(arg_keys[2], (NPAIRS * SLOTS, NTH), (4 * NPAIRS * (LMAX + 1)) ** -0.5, 0.046875, ((0, 8),)),
        "analysis_table": centred(arg_keys[3], (NPAIRS * SLOTS, NTH), 1.0, 6.0, ((0, 8),)),
        "pair_index": draw_pair_index(jax.random.fold_in(arg_keys[6], 71), 0),
        "diffusivity": jnp.clip(jnp.exp(jax.random.uniform(arg_keys[5], (4,), jnp.float32, math.log(0.0001), math.log(0.0004))), 0.0001, 0.0004),
    }


ROTATION = 2.0
SHELL_RADIUS = 16.0

def slot_layout(pair_values):
    slot_index = jnp.arange(SLOTS, dtype=jnp.int32)[None, :]
    lowest = pair_values.astype(jnp.int32)[:, None]
    first_part = slot_index < LMAX + 1 - lowest
    second_part = jnp.logical_and(jnp.logical_not(first_part), slot_index < LMAX + 2)
    degree = jnp.where(first_part, lowest + slot_index, slot_index - 1)
    wave_order = jnp.where(first_part, lowest, LMAX - lowest)
    return (first_part, second_part, degree, wave_order)

def fourier_tables(pair_values):
    lowest = pair_values.astype(jnp.int32)
    orders = jnp.stack([lowest, LMAX - lowest], axis=1)
    angle_step = jnp.arange(NPHI, dtype=jnp.int32)
    phases = orders[:, :, None] * angle_step[None, None, :] % NPHI
    angles = phases.astype(jnp.float32) * (2.0 * math.pi / NPHI)
    weight_order = jnp.where(orders == 0, 1.0, 2.0).astype(jnp.float32)[:, :, None]
    cosine = jnp.cos(angles)
    sine_part = jnp.sin(angles)
    synthesis = jnp.stack([weight_order * cosine, -weight_order * sine_part]).astype(jnp.bfloat16)
    analysis_fourier = (jnp.stack([cosine, -sine_part]) / NPHI).astype(jnp.bfloat16)
    return (synthesis, analysis_fourier)

def grid_products(grid_values):
    stream_theta, stream_phi, poloidal_theta, poloidal_phi = (grid_values[0], grid_values[1], grid_values[2], grid_values[3])
    thermal_theta, thermal_phi, magnetic_theta, magnetic_phi = (grid_values[4], grid_values[5], grid_values[6], grid_values[7])
    flow_theta = poloidal_theta - stream_phi
    flow_phi = poloidal_phi + stream_theta
    field_theta = -magnetic_phi
    field_phi = magnetic_theta
    stress = field_theta * field_phi - flow_theta * flow_phi
    pressure = 0.5 * (field_phi * field_phi - field_theta * field_theta) - 0.5 * (flow_phi * flow_phi - flow_theta * flow_theta)
    heat_flux = -(flow_theta * thermal_theta + flow_phi * thermal_phi)
    induction = -(flow_theta * field_phi - flow_phi * field_theta)
    return jnp.stack([stress, pressure, heat_flux, induction])

def coupled(source, partner, parity, degree, wave_order, alive):
    degree_real = degree.astype(jnp.float32)
    order_real = wave_order.astype(jnp.float32)
    lower_coupling = jnp.sqrt((degree_real * degree_real - order_real * order_real) * alive / jnp.maximum(4.0 * degree_real * degree_real - 1.0, 1.0))
    upper_degree = degree_real + 1.0
    upper_coupling = jnp.sqrt((upper_degree * upper_degree - order_real * order_real) / (4.0 * upper_degree * upper_degree - 1.0)) * alive * (degree < LMAX).astype(jnp.float32)
    spin_term = order_real / (degree_real * (degree_real + 1.0) + 2.0)
    turned = jnp.stack([-source[1], source[0]])
    below_slot = jnp.concatenate([jnp.zeros_like(partner[..., :1]), partner[..., :-1]], axis=-1)
    above_slot = jnp.concatenate([partner[..., 1:], jnp.zeros_like(partner[..., :1])], axis=-1)
    return ROTATION * (spin_term * turned + parity * (lower_coupling * below_slot + upper_coupling * above_slot))

def radial_solve(right_side, degree_flat, diffusivity):
    points = right_side.shape[2]
    counter = jnp.arange(1, points + 1, dtype=jnp.int32)
    product = counter[:, None] * counter[None, :] % (2 * (points + 1))
    sine_basis = math.sqrt(2.0 / (points + 1)) * jnp.sin(product.astype(jnp.float32) * (math.pi / (points + 1)))
    eigenvalues = 4.0 * (points + 1) * (points + 1) * jnp.sin(counter.astype(jnp.float32) * (math.pi / (2 * (points + 1)))) ** 2
    degree_real = degree_flat.astype(jnp.float32)
    horizontal = degree_real * (degree_real + 1.0) / (SHELL_RADIUS * SHELL_RADIUS)
    modal_part = jnp.einsum('jk,fcks->fcjs', sine_basis, right_side, precision=lax.Precision.HIGHEST)
    factor = 1.0 + diffusivity[:, None, None, None] * (eigenvalues[None, None, :, None] + horizontal[None, None, None, :])
    return jnp.einsum('jk,fcks->fcjs', sine_basis, modal_part / factor, precision=lax.Precision.HIGHEST)

def reference(spectra, dtheta_table, dphi_table, analysis_table, pair_index, diffusivity):
    first_part, second_part, degree, wave_order = slot_layout(pair_index)
    alive = jnp.logical_or(first_part, second_part).astype(jnp.float32)
    part_masks = jnp.stack([first_part, second_part], axis=1).astype(jnp.float32)
    masked_state = spectra.reshape(4, 2, NR, NPAIRS, SLOTS) * alive
    coeffs = masked_state.astype(jnp.bfloat16)
    spread = coeffs.astype(jnp.float32)[:, :, :, :, None, :] * part_masks[None, None, None]
    theta_rows = dtheta_table.reshape(NPAIRS, SLOTS, NTH).astype(jnp.float32)
    phi_rows = dphi_table.reshape(NPAIRS, SLOTS, NTH).astype(jnp.float32)
    along_theta = jnp.einsum('fcrpjs,pst->fcrpjt', spread, theta_rows)
    phi_direct = jnp.einsum('fcrpjs,pst->fcrpjt', spread, phi_rows)
    along_phi = jnp.stack([-phi_direct[:, 1], phi_direct[:, 0]], axis=1)
    grid_spectra = jnp.stack([along_theta, along_phi], axis=1)
    grid_spectra = jnp.transpose(grid_spectra, (3, 0, 1, 2, 4, 5, 6)).reshape(NR, 8, 2, NPAIRS, 2, NTH).astype(jnp.bfloat16)
    synthesis, analysis_fourier = fourier_tables(pair_index)
    synthesis_real = synthesis.astype(jnp.float32)
    analysis_real = analysis_fourier.astype(jnp.float32)

    def one_radius(radius_block):
        grid_values = jnp.einsum('qcpjt,cpjk->qtk', radius_block.astype(jnp.float32), synthesis_real)
        products = grid_products(grid_values).astype(jnp.bfloat16)
        return jnp.einsum('ftk,cpjk->fcpjt', products.astype(jnp.float32), analysis_real).astype(jnp.bfloat16)
    returned = lax.map(one_radius, grid_spectra)
    analysis_rows = analysis_table.reshape(NPAIRS, SLOTS, NTH).astype(jnp.float32)
    projected = jnp.einsum('rfcpjt,pst->fcrpjs', returned.astype(jnp.float32), analysis_rows)
    nonlinear = lax.optimization_barrier(jnp.sum(projected * part_masks[None, None, None], axis=4))
    forcing = jnp.stack([coupled(masked_state[0], masked_state[1], 1.0, degree, wave_order, alive), coupled(masked_state[1], masked_state[0], -1.0, degree, wave_order, alive)])
    forcing = jnp.concatenate([forcing, jnp.zeros_like(forcing)], axis=0)
    right_side = (masked_state + nonlinear + forcing) * alive
    solved = radial_solve(right_side.reshape(4, 2, NR, NPAIRS * SLOTS), degree.reshape(NPAIRS * SLOTS), diffusivity)
    return solved * alive.reshape(NPAIRS * SLOTS)
```

```python
import functools

import jax
import jax.numpy as jnp
from jax import lax
from jax.experimental import pallas as pl
from jax.experimental.pallas import tpu as pltpu
from jax.sharding import PartitionSpec as P

LMAX = 511
ROTATION = 2.0
SHELL_RADIUS = 16.0
RADII = 8
FAR = 1 << 20
VMEM_LIMIT = 48 * 1024 * 1024


def slot_rows(lowest, slots):
    slot = lax.broadcasted_iota(jnp.int32, (1, slots), 1)
    first = slot < LMAX + 1 - lowest
    held = slot < LMAX + 2
    second = jnp.logical_and(jnp.logical_not(first), held)
    degree = jnp.where(first, lowest + slot, slot - 1)
    order = jnp.where(first, lowest, LMAX - lowest)
    return first, second, held, degree, order


def greet(axis_sizes):
    barrier = pltpu.get_barrier_semaphore()
    total = 0
    for axis, size in axis_sizes:
        me = lax.axis_index(axis)
        for k in range(1, size):
            pl.semaphore_signal(
                barrier, inc=1, device_id={axis: lax.rem(me + k, size)},
                device_id_type=pl.DeviceIdType.MESH,
            )
        total += size - 1
    pl.semaphore_wait(barrier, total)


def forward_kernel(n, pair, spectra, dtheta, dphi, out, send, send_sem, recv_sem):
    greet([("ma", n)])
    me = lax.axis_index("ma")
    slots = spectra.shape[3]
    radii = RADII
    halves = n * radii // spectra.shape[2]
    width = dtheta.shape[1] // halves
    lowest = pair[me]
    first, second, _, _, _ = slot_rows(lowest, slots)
    keep = jnp.where(lowest == 0, 0.0, 1.0).astype(jnp.float32)

    def block_for(e):
        group = e // halves
        half = lax.rem(e, halves)
        x = spectra[:, :, pl.ds(pl.multiple_of(group * radii, radii), radii), :]
        x = x.reshape(8 * radii, slots)
        lhs = jnp.concatenate([jnp.where(first, x, 0.0), jnp.where(second, x, 0.0)], axis=0)
        lhs = lhs.astype(jnp.bfloat16)
        columns = pl.ds(pl.multiple_of(half * width, 128), width)
        t = jnp.dot(lhs, dtheta[:, columns], preferred_element_type=jnp.float32)
        d = jnp.dot(lhs, dphi[:, columns], preferred_element_type=jnp.float32)
        t = t.reshape(2, 4, 2, radii, width)
        d = d.reshape(2, 4, 2, radii, width)
        parts = []
        for j in range(2):
            z_t, w_t, s_t, a_t = (t[j, f] for f in range(4))
            z_d, w_d, s_d, a_d = (d[j, f] for f in range(4))
            pieces = [
                (w_t[0] + z_d[1], w_t[1] - z_d[0]),
                (z_t[0] - w_d[1], z_t[1] + w_d[0]),
                (s_t[0], s_t[1]),
                (-s_d[1], s_d[0]),
                (a_d[1], -a_d[0]),
                (a_t[0], a_t[1]),
            ]
            for real, imag in pieces:
                parts += [real, imag * keep if j == 0 else imag]
        return jnp.concatenate(parts, axis=0).astype(jnp.bfloat16)

    def copy_to(e, source):
        return pltpu.make_async_remote_copy(
            src_ref=send.at[e], dst_ref=out.at[source],
            send_sem=send_sem.at[e], recv_sem=recv_sem.at[source],
            device_id={"ma": e}, device_id_type=pl.DeviceIdType.MESH,
        )

    def push(k, carry):
        e = lax.rem(me + k, n)
        send[e] = block_for(e)
        copy_to(e, me).start()
        return carry

    lax.fori_loop(1, n, push, 0)
    out[me] = block_for(me)

    def finish(k, carry):
        e = lax.rem(me + k, n)
        source = lax.rem(me + n - k, n)
        copy_to(e, source).wait_send()
        copy_to(e, source).wait_recv()
        return carry

    lax.fori_loop(1, n, finish, 0)


def triad_kernel(n, partner, x, out, states, list_a, list_b):
    orders = 2 * n
    signed = 2 * orders
    radii, width = states.shape[2], states.shape[3]

    def unpack(g, carry):
        block = x[g].astype(jnp.float32).reshape(2, 6, 2, radii, width)
        for j in range(2):
            for q in range(6):
                real, imag = block[j, q, 0], block[j, q, 1]
                states[2 * g + j, 2 * q] = real
                states[2 * g + j, 2 * q + 1] = imag
                states[orders + 2 * g + j, 2 * q] = real
                states[orders + 2 * g + j, 2 * q + 1] = -imag
        return carry

    lax.fori_loop(0, n, unpack, 0)

    def one_order(t, carry):
        def gather(s, count):
            b = partner[t * signed + s]
            list_a[count] = s
            list_b[count] = b
            return count + jnp.where(b >= 0, 1, 0)

        count = lax.fori_loop(0, signed, gather, 0, unroll=8)

        def add(i, total):
            a, b = list_a[i], list_b[i]

            def mul(p, q):
                pr, pi = states[a, 2 * p], states[a, 2 * p + 1]
                qr, qi = states[b, 2 * q], states[b, 2 * q + 1]
                return pr * qr - pi * qi, pr * qi + pi * qr

            ut, up, st, sp, bt, bp = range(6)
            plan = (
                ((bt, bp, 1), (ut, up, -1)),
                ((bp, bp, 1), (bt, bt, -1), (up, up, -1), (ut, ut, 1)),
                ((ut, st, 1), (up, sp, 1)),
                ((ut, bp, 1), (up, bt, -1)),
            )
            new = list(total)
            for f, terms in enumerate(plan):
                for p, q, sign in terms:
                    real, imag = mul(p, q)
                    if sign > 0:
                        new[2 * f] += real
                        new[2 * f + 1] += imag
                    else:
                        new[2 * f] -= real
                        new[2 * f + 1] -= imag
            return tuple(new)

        zero = jnp.zeros((radii, width), jnp.float32)
        total = lax.fori_loop(0, count, add, (zero,) * 8)
        scale = (1.0, 1.0, 0.5, 0.5, -1.0, -1.0, -1.0, -1.0)
        rows = jnp.concatenate([v * c for v, c in zip(total, scale)], axis=0)
        out[t] = rows.astype(jnp.bfloat16)
        return carry

    lax.fori_loop(0, orders, one_order, 0)


def backward_kernel(
    n, rows_count, pair, diffusivity, y, spectra, analysis, out,
    got, edges, right, send_sem, recv_sem, edge_send, edge_recv,
):
    greet([("ma", n), ("row", rows_count)])
    me = lax.axis_index("ma")
    row = lax.axis_index("row")
    slots = spectra.shape[3]
    points = spectra.shape[2]
    radii = RADII
    groups = points // radii
    halves = n // groups
    width = analysis.shape[1] // halves

    def copy_to(e, source):
        return pltpu.make_async_remote_copy(
            src_ref=y.at[e], dst_ref=got.at[source],
            send_sem=send_sem.at[e], recv_sem=recv_sem.at[source],
            device_id={"ma": e}, device_id_type=pl.DeviceIdType.MESH,
        )

    def push(k, carry):
        e = lax.rem(me + k, n)
        copy_to(e, me).start()
        return carry

    lax.fori_loop(1, n, push, 0)
    got[me] = y[me]

    lowest = pair[me]
    first, second, held, degree, order = slot_rows(lowest, slots)
    alive = held.astype(jnp.float32)
    l = degree.astype(jnp.float32)
    m = order.astype(jnp.float32)
    lower = jnp.sqrt((l * l - m * m) * alive / jnp.maximum(4.0 * l * l - 1.0, 1.0)) * ROTATION
    u = l + 1.0
    upper = jnp.sqrt(jnp.maximum((u * u - m * m) / (4.0 * u * u - 1.0), 0.0))
    upper = jnp.where(degree < LMAX, upper * alive, 0.0) * ROTATION
    spin = ROTATION * m / (l * (l + 1.0) + 2.0) * alive

    def couple(v):
        edge = jnp.zeros((points, 1), jnp.float32)
        below = jnp.concatenate([edge, v[:, : slots - 1]], axis=1)
        above = jnp.concatenate([v[:, 1:], edge], axis=1)
        return lower * below + upper * above

    z0, z1 = (jnp.where(held, spectra[0, c], 0.0) for c in range(2))
    w0, w1 = (jnp.where(held, spectra[1, c], 0.0) for c in range(2))
    right[0, 0] = z0 - spin * z1 + couple(w0) * alive
    right[0, 1] = z1 + spin * z0 + couple(w1) * alive
    right[1, 0] = w0 - spin * w1 - couple(z0) * alive
    right[1, 1] = w1 + spin * w0 - couple(z1) * alive
    for f in (2, 3):
        for c in range(2):
            right[f, c] = jnp.where(held, spectra[f, c], 0.0)

    all_points = points * rows_count
    rho, log_rho, inner = [], [], []
    for f in range(4):
        off = diffusivity[f] * float((all_points + 1) ** 2)
        half_excess = (1.0 + diffusivity[f] * (l * (l + 1.0) / SHELL_RADIUS**2)) / (2.0 * off)
        root = jnp.sqrt(half_excess * half_excess + 2.0 * half_excess)
        inverse = 1.0 + half_excess + root
        rho.append(1.0 / inverse)
        log_rho.append(-jnp.log(inverse))
        inner.append(1.0 / (2.0 * off * root))
    at = lax.broadcasted_iota(jnp.int32, (points, slots), 0)

    def finish(source):
        @pl.when(source != me)
        def _():
            copy_to(source, source).wait_recv()

    contract = (((1,), (1,)), ((), ()))
    for g in range(groups):
        total = jnp.zeros((16 * radii, slots), jnp.float32)
        for h in range(halves):
            finish(halves * g + h)
            total += lax.dot_general(
                got[halves * g + h].reshape(16 * radii, width),
                analysis[:, h * width : (h + 1) * width],
                contract, preferred_element_type=jnp.float32,
            )
        total = total.reshape(2, 4, 2, radii, slots)
        added = jnp.where(first, total[0], jnp.where(second, total[1], 0.0))
        right[:, :, g * radii : (g + 1) * radii, :] += added

    last, start = [], []
    for f in range(4):
        for c in range(2):
            b = right[f, c]
            ahead, back = b, b
            power = rho[f]
            step = 1
            while step < points:
                ahead += power * jnp.where(at >= step, pltpu.roll(ahead, step, 0), 0.0)
                back += power * jnp.where(
                    at < points - step, pltpu.roll(back, points - step, 0), 0.0
                )
                power = power * power
                step *= 2
            right[f, c] = inner[f] * (ahead + back - b)
            last.append(ahead[points - 1 : points])
            start.append(back[0:1])
    edges[row] = jnp.concatenate(last + start, axis=0)

    def edge_copy(e, source):
        return pltpu.make_async_remote_copy(
            src_ref=edges.at[row], dst_ref=edges.at[source],
            send_sem=edge_send.at[e], recv_sem=edge_recv.at[source],
            device_id={"row": e}, device_id_type=pl.DeviceIdType.MESH,
        )

    for k in range(1, rows_count):
        edge_copy(lax.rem(row + k, rows_count), row).start()

    def drain(k, carry):
        copy_to(lax.rem(me + k, n), me).wait_send()
        return carry

    lax.fori_loop(1, n, drain, 0)
    for k in range(1, rows_count):
        edge_copy(lax.rem(row + k, rows_count), lax.rem(row + rows_count - k, rows_count)).wait()

    ahead_in = [0.0] * 4
    back_in = [0.0] * 4
    ahead_all = [0.0] * 4
    back_all = [0.0] * 4
    for e in range(rows_count):
        block = edges[e]
        for f in range(4):
            f_e = block[2 * f : 2 * f + 2]
            g_e = block[8 + 2 * f : 10 + 2 * f]
            gap = (row - 1 - e) * points
            weight = jnp.where(gap >= 0, jnp.exp(log_rho[f] * jnp.maximum(gap, 0).astype(jnp.float32)), 0.0)
            ahead_in[f] += weight * f_e
            gap = (e - row - 1) * points
            weight = jnp.where(gap >= 0, jnp.exp(log_rho[f] * jnp.maximum(gap, 0).astype(jnp.float32)), 0.0)
            back_in[f] += weight * g_e
            ahead_all[f] += jnp.exp(log_rho[f] * float((rows_count - 1 - e) * points)) * f_e
            back_all[f] += jnp.exp(log_rho[f] * float(e * points)) * g_e
    near = (at + 1).astype(jnp.float32)
    far = (points - at).astype(jnp.float32)
    for f in range(4):
        span = jnp.exp(log_rho[f] * float(all_points + 1))
        low = inner[f] * rho[f] * back_all[f]
        high = inner[f] * rho[f] * ahead_all[f]
        scale = 1.0 / (1.0 - span * span)
        alpha = (span * high - low) * scale
        beta = (span * low - high) * scale
        before = (row * points).astype(jnp.float32)
        after = ((rows_count - 1 - row) * points).astype(jnp.float32)
        left = inner[f] * ahead_in[f] + alpha * jnp.exp(log_rho[f] * before)
        rest = inner[f] * back_in[f] + beta * jnp.exp(log_rho[f] * after)
        rise = jnp.exp(log_rho[f] * near)
        fall = jnp.exp(log_rho[f] * far)
        for c in range(2):
            value = right[f, c] + left[c : c + 1] * rise + rest[c : c + 1] * fall
            out[f, c] = jnp.where(held, value, 0.0)


def triad_table(pair_index):
    orders = jnp.stack([pair_index, LMAX - pair_index], axis=1).reshape(-1)
    signed = jnp.concatenate([orders, jnp.where(orders == 0, FAR, -orders)])
    need = orders[:, None] - signed[None, :]
    match = need[:, :, None] == signed[None, None, :]
    at = jnp.arange(signed.shape[0], dtype=jnp.int32) + 1
    return (jnp.sum(jnp.where(match, at, 0), axis=2) - 1).reshape(-1)


def local(n, rows_count, spectra, dtheta, dphi, analysis, pair_index, diffusivity):
    points, slots = spectra.shape[2], spectra.shape[3]
    radii = RADII
    halves = n * radii // points
    width = -(-dtheta.shape[1] // (128 * halves)) * 128
    extra = width * halves - dtheta.shape[1]
    if extra:
        dtheta, dphi, analysis = (jnp.pad(v, ((0, 0), (0, extra))) for v in (dtheta, dphi, analysis))
    vmem = pl.BlockSpec(memory_space=pltpu.VMEM)
    smem = pl.BlockSpec(memory_space=pltpu.SMEM)
    partner = triad_table(pair_index)
    grid = pl.pallas_call(
        functools.partial(forward_kernel, n),
        out_shape=jax.ShapeDtypeStruct((n, 24 * radii, width), jnp.bfloat16),
        in_specs=[smem, vmem, vmem, vmem],
        out_specs=vmem,
        scratch_shapes=[
            pltpu.VMEM((n, 24 * radii, width), jnp.bfloat16),
            pltpu.SemaphoreType.DMA((n,)),
            pltpu.SemaphoreType.DMA((n,)),
        ],
        compiler_params=pltpu.CompilerParams(
            collective_id=0, has_side_effects=True, vmem_limit_bytes=VMEM_LIMIT
        ),
        name="forward",
    )(pair_index, spectra, dtheta, dphi)
    products = pl.pallas_call(
        functools.partial(triad_kernel, n),
        out_shape=jax.ShapeDtypeStruct((2 * n, 8 * radii, width), jnp.bfloat16),
        in_specs=[smem, vmem],
        out_specs=vmem,
        scratch_shapes=[
            pltpu.VMEM((4 * n, 12, radii, width), jnp.float32),
            pltpu.SMEM((4 * n + 8,), jnp.int32),
            pltpu.SMEM((4 * n + 8,), jnp.int32),
        ],
        compiler_params=pltpu.CompilerParams(vmem_limit_bytes=VMEM_LIMIT),
        name="triads",
    )(partner, grid)
    products = products.reshape(n, 16 * radii, width)
    return pl.pallas_call(
        functools.partial(backward_kernel, n, rows_count),
        out_shape=jax.ShapeDtypeStruct(spectra.shape, jnp.float32),
        in_specs=[smem, smem, vmem, vmem, vmem],
        out_specs=vmem,
        scratch_shapes=[
            pltpu.VMEM((n, 16 * radii, width), jnp.bfloat16),
            pltpu.VMEM((rows_count, 16, slots), jnp.float32),
            pltpu.VMEM(spectra.shape, jnp.float32),
            pltpu.SemaphoreType.DMA((n,)),
            pltpu.SemaphoreType.DMA((n,)),
            pltpu.SemaphoreType.DMA((rows_count,)),
            pltpu.SemaphoreType.DMA((rows_count,)),
        ],
        compiler_params=pltpu.CompilerParams(
            collective_id=1, has_side_effects=True, vmem_limit_bytes=VMEM_LIMIT
        ),
        name="backward",
    )(pair_index, diffusivity, products, spectra, analysis)


def solution(mesh):
    n, rows_count = mesh.shape["ma"], mesh.shape["row"]
    return jax.shard_map(
        functools.partial(local, n, rows_count),
        mesh=mesh,
        in_specs=(
            P(None, None, "row", "ma"),
            P("ma", None),
            P("ma", None),
            P("ma", None),
            P(),
            P(),
        ),
        out_specs=P(None, None, "row", "ma"),
        check_vma=False,
    )
```

```python
import functools

import jax
import jax.numpy as jnp
from jax import lax
from jax.experimental import pallas as pl
from jax.experimental.pallas import tpu as pltpu
from jax.sharding import PartitionSpec as P

LMAX = 511
ROTATION = 2.0
SHELL_RADIUS = 16.0
RADII = 8
FAR = 1 << 20
VMEM_LIMIT = 48 * 1024 * 1024


def slot_rows(lowest, slots):
    slot = lax.broadcasted_iota(jnp.int32, (1, slots), 1)
    first = slot < LMAX + 1 - lowest
    held = slot < LMAX + 2
    second = jnp.logical_and(jnp.logical_not(first), held)
    degree = jnp.where(first, lowest + slot, slot - 1)
    order = jnp.where(first, lowest, LMAX - lowest)
    return first, second, held, degree, order


def greet(axis_sizes):
    barrier = pltpu.get_barrier_semaphore()
    total = 0
    for axis, size in axis_sizes:
        me = lax.axis_index(axis)
        for k in range(1, size):
            pl.semaphore_signal(
                barrier, inc=1, device_id={axis: lax.rem(me + k, size)},
                device_id_type=pl.DeviceIdType.MESH,
            )
        total += size - 1
    pl.semaphore_wait(barrier, total)


def ring(me, n):
    tall = n // 4

    def target(dy, dx, dc):
        y, x, c = me // 4, lax.rem(me // 2, 2), lax.rem(me, 2)
        return lax.rem(y + dy, tall) * 4 + lax.rem(x + dx, 2) * 2 + lax.rem(c + dc, 2)

    return target


def far_first(n):
    steps = [(dy, dx, dc) for dy in range(n // 4) for dx in range(2) for dc in range(2)]
    return sorted(steps[1:], key=lambda d: (-((d[0] > 0) + d[1]), d[2], d[1]))


def forward_kernel(
    n, pair, spectra_hbm, dtheta_hbm, dphi_hbm, out, triads,
    spectra, dtheta, dphi, send, load_sem, send_sem, recv_sem,
):
    loads = [
        pltpu.make_async_copy(spectra_hbm, spectra, load_sem.at[0]),
        pltpu.make_async_copy(dtheta_hbm, dtheta, load_sem.at[1]),
        pltpu.make_async_copy(dphi_hbm, dphi, load_sem.at[2]),
    ]
    for load in loads:
        load.start()
    greet([("ma", n)])
    me = lax.axis_index("ma")
    slots = spectra.shape[3]
    radii = RADII
    halves = n * radii // spectra.shape[2]
    width = dtheta.shape[1] // halves
    lowest = pair[me]
    first, second, _, _, _ = slot_rows(lowest, slots)
    keep = jnp.where(lowest == 0, 0.0, 1.0).astype(jnp.float32)
    for load in loads:
        load.wait()

    def block_for(e):
        group = e // halves
        half = lax.rem(e, halves)
        x = spectra[:, :, pl.ds(pl.multiple_of(group * radii, radii), radii), :]
        x = x.reshape(8 * radii, slots)
        lhs = jnp.concatenate([jnp.where(first, x, 0.0), jnp.where(second, x, 0.0)], axis=0)
        lhs = lhs.astype(jnp.bfloat16)
        columns = pl.ds(pl.multiple_of(half * width, 128), width)
        t = jnp.dot(lhs, dtheta[:, columns], preferred_element_type=jnp.float32)
        d = jnp.dot(lhs, dphi[:, columns], preferred_element_type=jnp.float32)
        t = t.reshape(2, 4, 2, radii, width)
        d = d.reshape(2, 4, 2, radii, width)
        parts = []
        for j in range(2):
            z_t, w_t, s_t, a_t = (t[j, f] for f in range(4))
            z_d, w_d, s_d, a_d = (d[j, f] for f in range(4))
            pieces = [
                (w_t[0] + z_d[1], w_t[1] - z_d[0]),
                (z_t[0] - w_d[1], z_t[1] + w_d[0]),
                (s_t[0], s_t[1]),
                (-s_d[1], s_d[0]),
                (a_d[1], -a_d[0]),
                (a_t[0], a_t[1]),
            ]
            for real, imag in pieces:
                parts += [real, imag * keep if j == 0 else imag]
        return jnp.concatenate(parts, axis=0).astype(jnp.bfloat16)

    def copy_to(e, source):
        return pltpu.make_async_remote_copy(
            src_ref=send.at[e], dst_ref=out.at[source],
            send_sem=send_sem.at[e], recv_sem=recv_sem.at[source],
            device_id={"ma": e}, device_id_type=pl.DeviceIdType.MESH,
        )

    target = ring(me, n)
    for step in far_first(n):
        e = target(*step)
        send[e] = block_for(e)
        copy_to(e, me).start()
    out[me] = block_for(me)
    list_triads(n, pair, triads)

    def finish(k, carry):
        e = lax.rem(me + k, n)
        copy_to(e, e).wait_send()
        copy_to(e, e).wait_recv()
        return carry

    lax.fori_loop(1, n, finish, 0)


def list_triads(n, pair, triads):
    orders, signed = 2 * n, 4 * n

    def signed_orders(shape, dim, parts):
        index = lax.broadcasted_iota(jnp.int32, shape, dim)
        place = lax.rem(index, orders)
        value = jnp.zeros(shape, jnp.int32)
        for g in range(n):
            value = jnp.where(place == 2 * g, pair[g], value)
            value = jnp.where(place == 2 * g + 1, LMAX - pair[g], value)
        if parts == 1:
            return value
        value = jnp.where(index >= orders, jnp.where(value == 0, FAR, -value), value)
        return jnp.where(index < signed, value, 3 * FAR)

    as_b = signed_orders((signed, 1), 0, 2)
    as_a = signed_orders((1, 128), 1, 2)
    as_m = signed_orders((orders, 1), 0, 1)
    need = as_m - as_a
    found = jnp.zeros((orders, 128), jnp.float32)
    for s in range(signed):
        found = jnp.where(need == as_b[s : s + 1, :], float(s + 1), found)
    valid = found > 0.0
    earlier = lax.broadcasted_iota(jnp.int32, (128, 128), 0) < lax.broadcasted_iota(
        jnp.int32, (128, 128), 1
    )
    ones = jnp.where(valid, 1.0, 0.0)
    rank = jnp.dot(
        ones.astype(jnp.bfloat16), jnp.where(earlier, 1.0, 0.0).astype(jnp.bfloat16),
        preferred_element_type=jnp.float32,
    )
    lane = lax.broadcasted_iota(jnp.int32, (orders, 128), 1)
    code = lane.astype(jnp.float32) * float(signed) + found - 1.0
    rank = jnp.where(valid, rank, -1.0)

    def place(s, table):
        hit = jnp.sum(jnp.where(rank == s.astype(jnp.float32), code, 0.0), axis=1, keepdims=True)
        return jnp.where(lane == s, hit, table)

    table = lax.fori_loop(0, signed, place, jnp.zeros((orders, 128), jnp.float32))
    triads[:, :128] = table.astype(jnp.int32)
    count = jnp.sum(ones, axis=1, keepdims=True)
    triads[:, 128:] = jnp.broadcast_to(count, (orders, 128)).astype(jnp.int32)


def triad_kernel(n, triads, x, out, states):
    orders = 2 * n
    signed = 2 * orders
    shift = signed.bit_length() - 1
    radii, width = states.shape[2], states.shape[3]

    def unpack(g, carry):
        block = x[g].astype(jnp.float32).reshape(2, 6, 2, radii, width)
        for j in range(2):
            for q in range(6):
                real, imag = block[j, q, 0], block[j, q, 1]
                states[2 * g + j, 2 * q] = real
                states[2 * g + j, 2 * q + 1] = imag
                states[orders + 2 * g + j, 2 * q] = real
                states[orders + 2 * g + j, 2 * q + 1] = -imag
        return carry

    lax.fori_loop(0, n, unpack, 0)

    def one_order(t, carry):
        count = triads[t, 128]

        def add(i, total):
            code = triads[t, i]
            a = lax.shift_right_logical(code, shift)
            b = code - a * signed

            def mul(p, q):
                pr, pi = states[a, 2 * p], states[a, 2 * p + 1]
                qr, qi = states[b, 2 * q], states[b, 2 * q + 1]
                return pr * qr - pi * qi, pr * qi + pi * qr

            ut, up, st, sp, bt, bp = range(6)
            plan = (
                ((bt, bp, 1), (ut, up, -1)),
                ((bp, bp, 1), (bt, bt, -1), (up, up, -1), (ut, ut, 1)),
                ((ut, st, 1), (up, sp, 1)),
                ((ut, bp, 1), (up, bt, -1)),
            )
            new = list(total)
            for f, terms in enumerate(plan):
                for p, q, sign in terms:
                    real, imag = mul(p, q)
                    if sign > 0:
                        new[2 * f] += real
                        new[2 * f + 1] += imag
                    else:
                        new[2 * f] -= real
                        new[2 * f + 1] -= imag
            return tuple(new)

        zero = jnp.zeros((radii, width), jnp.float32)
        total = lax.fori_loop(0, count, add, (zero,) * 8)
        scale = (1.0, 1.0, 0.5, 0.5, -1.0, -1.0, -1.0, -1.0)
        rows = jnp.concatenate([v * c for v, c in zip(total, scale)], axis=0)
        out[t] = rows.astype(jnp.bfloat16)
        return carry

    lax.fori_loop(0, orders, one_order, 0)


def backward_kernel(
    n, rows_count, pair, diffusivity, y, spectra_hbm, analysis_hbm, out,
    spectra, analysis, got, edges, right, carries,
    load_sem, send_sem, recv_sem, edge_send, edge_recv,
):
    loads = [
        pltpu.make_async_copy(spectra_hbm, spectra, load_sem.at[0]),
        pltpu.make_async_copy(analysis_hbm, analysis, load_sem.at[1]),
    ]
    for load in loads:
        load.start()
    greet([("ma", n), ("row", rows_count)])
    me = lax.axis_index("ma")
    row = lax.axis_index("row")
    slots = spectra.shape[3]
    points = spectra.shape[2]
    radii = RADII
    groups = points // radii
    halves = n // groups
    width = analysis.shape[1] // halves

    def copy_to(e, source):
        return pltpu.make_async_remote_copy(
            src_ref=y.at[e], dst_ref=got.at[source],
            send_sem=send_sem.at[e], recv_sem=recv_sem.at[source],
            device_id={"ma": e}, device_id_type=pl.DeviceIdType.MESH,
        )

    target = ring(me, n)
    for step in reversed(far_first(n)):
        copy_to(target(*step), me).start()
    got[me] = y[me]

    lowest = pair[me]
    first, second, held, degree, order = slot_rows(lowest, slots)
    alive = held.astype(jnp.float32)
    l = degree.astype(jnp.float32)
    m = order.astype(jnp.float32)
    lower = jnp.sqrt((l * l - m * m) * alive / jnp.maximum(4.0 * l * l - 1.0, 1.0)) * ROTATION
    u = l + 1.0
    upper = jnp.sqrt(jnp.maximum((u * u - m * m) / (4.0 * u * u - 1.0), 0.0))
    upper = jnp.where(degree < LMAX, upper * alive, 0.0) * ROTATION
    spin = ROTATION * m / (l * (l + 1.0) + 2.0) * alive

    all_points = points * rows_count
    field = lax.broadcasted_iota(jnp.int32, (8, 1), 0) // 2
    nu = jnp.zeros((8, 1), jnp.float32)
    for f in range(4):
        nu = jnp.where(field == f, diffusivity[f], nu)
    off = nu * float((all_points + 1) ** 2)
    half_excess = (1.0 + nu * (l * (l + 1.0) / SHELL_RADIUS**2)) / (2.0 * off)
    root = jnp.sqrt(half_excess * half_excess + 2.0 * half_excess)
    inverse = 1.0 + half_excess + root
    rho = 1.0 / inverse
    log_rho = -jnp.log(inverse)
    inner = 1.0 / (2.0 * off * root)
    at = lax.broadcasted_iota(jnp.int32, (radii, slots), 0)
    near = (at + 1).astype(jnp.float32)
    far = (radii - at).astype(jnp.float32)

    def power(exponent):
        return jnp.exp(log_rho * exponent)

    for load in loads:
        load.wait()

    def couple(v):
        edge = jnp.zeros((points, 1), jnp.float32)
        below = jnp.concatenate([edge, v[:, : slots - 1]], axis=1)
        above = jnp.concatenate([v[:, 1:], edge], axis=1)
        return lower * below + upper * above

    z0, z1 = (jnp.where(held, spectra[0, c], 0.0) for c in range(2))
    w0, w1 = (jnp.where(held, spectra[1, c], 0.0) for c in range(2))
    right[0, 0] = z0 - spin * z1 + couple(w0) * alive
    right[0, 1] = z1 + spin * z0 + couple(w1) * alive
    right[1, 0] = w0 - spin * w1 - couple(z0) * alive
    right[1, 1] = w1 + spin * w0 - couple(z1) * alive
    for f in (2, 3):
        for c in range(2):
            right[f, c] = jnp.where(held, spectra[f, c], 0.0)

    contract = (((1,), (1,)), ((), ()))
    own_group = me // halves
    for k in group_order(n, groups):
        g = lax.rem(own_group // k[2] + k[0], groups // k[2]) * k[2] + lax.rem(
            lax.rem(own_group, k[2]) + k[1], k[2]
        )
        total = jnp.zeros((16 * radii, slots), jnp.float32)
        for h in range(halves):
            source = halves * g + h

            @pl.when(source != me)
            def _(source=source):
                copy_to(source, source).wait_recv()

            total += lax.dot_general(
                got[source], analysis[:, h * width : (h + 1) * width],
                contract, preferred_element_type=jnp.float32,
            )
        total = total.reshape(2, 4, 2, radii, slots)
        added = jnp.where(first, total[0], jnp.where(second, total[1], 0.0))
        rows = pl.ds(pl.multiple_of(g * radii, radii), radii)
        last, start = [], []
        for f in range(4):
            scale = inner[2 * f : 2 * f + 1]
            for c in range(2):
                b = right[f, c, rows, :] + added[f, c]
                ahead, back = b, b
                ratio = rho[2 * f : 2 * f + 1]
                step = 1
                while step < radii:
                    ahead += ratio * jnp.where(at >= step, pltpu.roll(ahead, step, 0), 0.0)
                    back += ratio * jnp.where(
                        at < radii - step, pltpu.roll(back, radii - step, 0), 0.0
                    )
                    ratio = ratio * ratio
                    step *= 2
                right[f, c, rows, :] = scale * (ahead + back - b)
                last.append(ahead[radii - 1 : radii])
                start.append(back[0:1])
        carries[g, 0] = jnp.concatenate(last, axis=0)
        carries[g, 1] = jnp.concatenate(start, axis=0)

    hop = power(float(radii))
    ahead_at, back_at = [], []
    total = jnp.zeros((8, slots), jnp.float32)
    for g in range(groups):
        ahead_at.append(total)
        total = hop * total + carries[g, 0]
    edges[row, 0:8] = total
    total = jnp.zeros((8, slots), jnp.float32)
    for g in reversed(range(groups)):
        back_at.insert(0, total)
        total = hop * total + carries[g, 1]
    edges[row, 8:16] = total

    def edge_copy(e, source):
        return pltpu.make_async_remote_copy(
            src_ref=edges.at[row], dst_ref=edges.at[source],
            send_sem=edge_send.at[e], recv_sem=edge_recv.at[source],
            device_id={"row": e}, device_id_type=pl.DeviceIdType.MESH,
        )

    for k in range(1, rows_count):
        edge_copy(lax.rem(row + k, rows_count), row).start()

    before = (row * points).astype(jnp.float32)
    after = ((rows_count - 1 - row) * points).astype(jnp.float32)
    span = power(float(all_points + 1))
    scale = 1.0 / (1.0 - span * span)
    to_start, to_end = power(before), power(after)
    rise = [jnp.exp(log_rho[2 * f : 2 * f + 1] * near) for f in range(4)]
    fall = [jnp.exp(log_rho[2 * f : 2 * f + 1] * far) for f in range(4)]
    shifts = [power(float(k * points)) for k in range(rows_count)]
    inside = [power(float(k * radii)) for k in range(groups)]

    def drain(k, carry):
        copy_to(lax.rem(me + k, n), me).wait_send()
        return carry

    lax.fori_loop(1, n, drain, 0)
    for k in range(1, rows_count):
        e = lax.rem(row + k, rows_count)
        edge_copy(e, e).wait()

    zero = jnp.zeros((8, slots), jnp.float32)
    ahead_in, back_in, ahead_all, back_all = zero, zero, zero, zero
    for e in range(rows_count):
        f_e, g_e = edges[e, 0:8], edges[e, 8:16]
        weight, reverse = zero, zero
        for k in range(rows_count - 1):
            weight = jnp.where(row - 1 - e == k, shifts[k], weight)
            reverse = jnp.where(e - row - 1 == k, shifts[k], reverse)
        ahead_in += weight * f_e
        back_in += reverse * g_e
        ahead_all += shifts[rows_count - 1 - e] * f_e
        back_all += shifts[e] * g_e
    low = inner * rho * back_all
    high = inner * rho * ahead_all
    left = inner * ahead_in + (span * high - low) * scale * to_start
    rest = inner * back_in + (span * low - high) * scale * to_end
    for g in range(groups):
        here = left * inside[g] + inner * ahead_at[g]
        there = rest * inside[groups - 1 - g] + inner * back_at[g]
        for f in range(4):
            for c in range(2):
                i = 2 * f + c
                value = right[f, c, g * radii : (g + 1) * radii, :]
                value = value + here[i : i + 1] * rise[f] + there[i : i + 1] * fall[f]
                out[f, c, g * radii : (g + 1) * radii, :] = jnp.where(held, value, 0.0)


def group_order(n, groups):
    inner = 2 if groups % 2 == 0 and n == 2 * groups else 1
    steps = [(dy, dx, inner) for dy in range(groups // inner) for dx in range(inner)]
    return sorted(steps, key=lambda d: (d[0] > 0) + d[1])


def local(n, rows_count, spectra, dtheta, dphi, analysis, pair_index, diffusivity):
    points, slots = spectra.shape[2], spectra.shape[3]
    radii = RADII
    halves = n * radii // points
    width = -(-dtheta.shape[1] // (128 * halves)) * 128
    extra = width * halves - dtheta.shape[1]
    if extra:
        dtheta, dphi, analysis = (jnp.pad(v, ((0, 0), (0, extra))) for v in (dtheta, dphi, analysis))
    vmem = pl.BlockSpec(memory_space=pltpu.VMEM)
    smem = pl.BlockSpec(memory_space=pltpu.SMEM)
    hbm = pl.BlockSpec(memory_space=pltpu.HBM)
    shape = spectra.shape
    table_shape = dtheta.shape
    grid, triads = pl.pallas_call(
        functools.partial(forward_kernel, n),
        out_shape=[
            jax.ShapeDtypeStruct((n, 24 * radii, width), jnp.bfloat16),
            jax.ShapeDtypeStruct((2 * n, 256), jnp.int32),
        ],
        in_specs=[smem, hbm, hbm, hbm],
        out_specs=[vmem, vmem],
        scratch_shapes=[
            pltpu.VMEM(shape, jnp.float32),
            pltpu.VMEM(table_shape, jnp.bfloat16),
            pltpu.VMEM(table_shape, jnp.bfloat16),
            pltpu.VMEM((n, 24 * radii, width), jnp.bfloat16),
            pltpu.SemaphoreType.DMA((3,)),
            pltpu.SemaphoreType.DMA((n,)),
            pltpu.SemaphoreType.DMA((n,)),
        ],
        compiler_params=pltpu.CompilerParams(
            collective_id=0, has_side_effects=True, vmem_limit_bytes=VMEM_LIMIT
        ),
        name="forward",
    )(pair_index, spectra, dtheta, dphi)
    products = pl.pallas_call(
        functools.partial(triad_kernel, n),
        out_shape=jax.ShapeDtypeStruct((2 * n, 8 * radii, width), jnp.bfloat16),
        in_specs=[smem, vmem],
        out_specs=vmem,
        scratch_shapes=[
            pltpu.VMEM((4 * n, 12, radii, width), jnp.float32),
        ],
        compiler_params=pltpu.CompilerParams(vmem_limit_bytes=VMEM_LIMIT),
        name="triads",
    )(triads, grid)
    products = products.reshape(n, 16 * radii, width)
    return pl.pallas_call(
        functools.partial(backward_kernel, n, rows_count),
        out_shape=jax.ShapeDtypeStruct(spectra.shape, jnp.float32),
        in_specs=[smem, smem, vmem, hbm, hbm],
        out_specs=vmem,
        scratch_shapes=[
            pltpu.VMEM(shape, jnp.float32),
            pltpu.VMEM(table_shape, jnp.bfloat16),
            pltpu.VMEM((n, 16 * radii, width), jnp.bfloat16),
            pltpu.VMEM((rows_count, 16, slots), jnp.float32),
            pltpu.VMEM(shape, jnp.float32),
            pltpu.VMEM((points // radii, 2, 8, slots), jnp.float32),
            pltpu.SemaphoreType.DMA((2,)),
            pltpu.SemaphoreType.DMA((n,)),
            pltpu.SemaphoreType.DMA((n,)),
            pltpu.SemaphoreType.DMA((rows_count,)),
            pltpu.SemaphoreType.DMA((rows_count,)),
        ],
        compiler_params=pltpu.CompilerParams(
            collective_id=1, has_side_effects=True, vmem_limit_bytes=VMEM_LIMIT
        ),
        name="backward",
    )(pair_index, diffusivity, products, spectra, analysis)


def solution(mesh):
    n, rows_count = mesh.shape["ma"], mesh.shape["row"]
    return jax.shard_map(
        functools.partial(local, n, rows_count),
        mesh=mesh,
        in_specs=(
            P(None, None, "row", "ma"),
            P("ma", None),
            P("ma", None),
            P("ma", None),
            P(),
            P(),
        ),
        out_specs=P(None, None, "row", "ma"),
        check_vma=False,
    )
```

```python
import functools

import jax
import jax.numpy as jnp
from jax import lax
from jax.experimental import pallas as pl
from jax.experimental.pallas import tpu as pltpu
from jax.sharding import PartitionSpec as P

LMAX = 511
ROTATION = 2.0
SHELL_RADIUS = 16.0
RADII = 8
VMEM_LIMIT = 62 * 1024 * 1024


def slot_rows(lowest, slots):
    slot = lax.broadcasted_iota(jnp.int32, (1, slots), 1)
    first = slot < LMAX + 1 - lowest
    held = slot < LMAX + 2
    second = jnp.logical_and(jnp.logical_not(first), held)
    degree = jnp.where(first, lowest + slot, slot - 1)
    order = jnp.where(first, lowest, LMAX - lowest)
    return first, second, held, degree, order


def greet(axis_sizes):
    barrier = pltpu.get_barrier_semaphore()
    total = 0
    for axis, size in axis_sizes:
        me = lax.axis_index(axis)
        for k in range(1, size):
            pl.semaphore_signal(
                barrier, inc=1, device_id={axis: lax.rem(me + k, size)},
                device_id_type=pl.DeviceIdType.MESH,
            )
        total += size - 1
    pl.semaphore_wait(barrier, total)


def ring(me, n):
    tall = n // 4

    def target(dy, dx, dc):
        y, x, c = me // 4, lax.rem(me // 2, 2), lax.rem(me, 2)
        return lax.rem(y + dy, tall) * 4 + lax.rem(x + dx, 2) * 2 + lax.rem(c + dc, 2)

    return target


def far_first(n):
    steps = [(dy, dx, dc) for dy in range(n // 4) for dx in range(2) for dc in range(2)]
    return sorted(steps[1:], key=lambda d: (-((d[0] > 0) + d[1]), d[2], d[1]))


def step_kernel(
    n, rows_count, partner, pair, diffusivity, spectra_hbm, dtheta_hbm, dphi_hbm, analysis_hbm, out,
    spectra, dtheta, dphi, analysis, send, x, states, sums, got, edges, right, carries,
    load_sem, send_sem, recv_sem, back_send, back_recv, edge_send, edge_recv,
):
    loads = [
        pltpu.make_async_copy(source, target, load_sem.at[i])
        for i, (source, target) in enumerate(
            [(spectra_hbm, spectra), (dtheta_hbm, dtheta), (dphi_hbm, dphi), (analysis_hbm, analysis)]
        )
    ]
    for load in loads:
        load.start()
    greet([("ma", n), ("row", rows_count)])
    me = lax.axis_index("ma")
    row = lax.axis_index("row")
    slots = spectra.shape[3]
    points = spectra.shape[2]
    radii = RADII
    groups = points // radii
    halves = n // groups
    width = dtheta.shape[1] // halves
    chunks = width // 128
    orders = 2 * n
    keep = jnp.where(pair[me] == 0, 0.0, 1.0).astype(jnp.float32)
    lowest = pair[me]
    first, second, held, degree, order = slot_rows(lowest, slots)
    alive = held.astype(jnp.float32)
    l = degree.astype(jnp.float32)
    m = order.astype(jnp.float32)
    lower = jnp.sqrt((l * l - m * m) * alive / jnp.maximum(4.0 * l * l - 1.0, 1.0)) * ROTATION
    u = l + 1.0
    upper = jnp.sqrt(jnp.maximum((u * u - m * m) / (4.0 * u * u - 1.0), 0.0))
    upper = jnp.where(degree < LMAX, upper * alive, 0.0) * ROTATION
    spin = ROTATION * m / (l * (l + 1.0) + 2.0) * alive

    all_points = points * rows_count
    field = lax.broadcasted_iota(jnp.int32, (8, 1), 0) // 2
    nu = jnp.zeros((8, 1), jnp.float32)
    for f in range(4):
        nu = jnp.where(field == f, diffusivity[f], nu)
    off = nu * float((all_points + 1) ** 2)
    half_excess = (1.0 + nu * (l * (l + 1.0) / SHELL_RADIUS**2)) / (2.0 * off)
    root = jnp.sqrt(half_excess * half_excess + 2.0 * half_excess)
    inverse = 1.0 + half_excess + root
    rho = 1.0 / inverse
    log_rho = -jnp.log(inverse)
    inner = 1.0 / (2.0 * off * root)
    at = lax.broadcasted_iota(jnp.int32, (radii, slots), 0)
    near = (at + 1).astype(jnp.float32)
    far = (radii - at).astype(jnp.float32)

    def power(exponent):
        return jnp.exp(log_rho * exponent)

    for load in loads[:3]:
        load.wait()

    def block_for(e):
        group = e // halves
        half = lax.rem(e, halves)
        x = spectra[:, :, pl.ds(pl.multiple_of(group * radii, radii), radii), :]
        x = x.reshape(8 * radii, slots)
        lhs = jnp.concatenate([jnp.where(first, x, 0.0), jnp.where(second, x, 0.0)], axis=0)
        lhs = lhs.astype(jnp.bfloat16)
        columns = pl.ds(pl.multiple_of(half * width, 128), width)
        t = jnp.dot(lhs, dtheta[:, columns], preferred_element_type=jnp.float32)
        d = jnp.dot(lhs, dphi[:, columns], preferred_element_type=jnp.float32)
        t = t.reshape(2, 4, 2, radii, width)
        d = d.reshape(2, 4, 2, radii, width)
        parts = []
        for j in range(2):
            z_t, w_t, s_t, a_t = (t[j, f] for f in range(4))
            z_d, w_d, s_d, a_d = (d[j, f] for f in range(4))
            pieces = [
                (w_t[0] + z_d[1], w_t[1] - z_d[0]),
                (z_t[0] - w_d[1], z_t[1] + w_d[0]),
                (s_t[0], s_t[1]),
                (-s_d[1], s_d[0]),
                (a_d[1], -a_d[0]),
                (a_t[0], a_t[1]),
            ]
            for real, imag in pieces:
                parts += [real, imag * keep if j == 0 else imag]
        return jnp.concatenate(parts, axis=0).astype(jnp.bfloat16)

    def grid_copy(e, source, c):
        return pltpu.make_async_remote_copy(
            src_ref=send.at[c, e], dst_ref=x.at[c, source],
            send_sem=send_sem.at[c, e], recv_sem=recv_sem.at[c, source],
            device_id={"ma": e}, device_id_type=pl.DeviceIdType.MESH,
        )

    def back_copy(e, source, c):
        return pltpu.make_async_remote_copy(
            src_ref=sums.at[c, e], dst_ref=got.at[c, source],
            send_sem=back_send.at[c, e], recv_sem=back_recv.at[c, source],
            device_id={"ma": e}, device_id_type=pl.DeviceIdType.MESH,
        )

    target = ring(me, n)
    for step in far_first(n):
        e = target(*step)
        value = block_for(e)
        for c in range(chunks):
            send[c, e] = value[:, c * 128 : (c + 1) * 128]
        grid_copy(e, me, 0).start()
    for c in range(1, chunks):
        for step in far_first(n):
            grid_copy(target(*step), me, c).start()
    value = block_for(me)
    for c in range(chunks):
        x[c, me] = value[:, c * 128 : (c + 1) * 128]

    def couple(v):
        edge = jnp.zeros((points, 1), jnp.float32)
        below = jnp.concatenate([edge, v[:, : slots - 1]], axis=1)
        above = jnp.concatenate([v[:, 1:], edge], axis=1)
        return lower * below + upper * above

    z0, z1 = (jnp.where(held, spectra[0, c], 0.0) for c in range(2))
    w0, w1 = (jnp.where(held, spectra[1, c], 0.0) for c in range(2))
    right[0, 0] = z0 - spin * z1 + couple(w0) * alive
    right[0, 1] = z1 + spin * z0 + couple(w1) * alive
    right[1, 0] = w0 - spin * w1 - couple(z0) * alive
    right[1, 1] = w1 + spin * w0 - couple(z1) * alive
    for f in (2, 3):
        for c in range(2):
            right[f, c] = jnp.where(held, spectra[f, c], 0.0)

    zero = jnp.zeros((radii, 128), jnp.float32)
    for q in range(12):
        states[3 * orders, q] = zero

    def chunk_step(c, carry):
        def arrive(k, carry):
            e = lax.rem(me + k, n)
            grid_copy(e, e, c).wait_recv()
            return carry

        lax.fori_loop(1, n, arrive, 0)

        def unpack(g, carry):
            block = x[c, g].astype(jnp.float32).reshape(2, 6, 2, radii, 128)
            for j in range(2):
                at_order = 2 * g + j
                u_t, u_p, s_t, s_p, b_t, b_p = (block[j, q] for q in range(6))
                for q, (p, t) in enumerate(((b_p, b_t), (u_p, u_t), (s_p, s_t))):
                    plus = (p[0] - t[1], p[1] + t[0])
                    minus = (p[0] + t[1], p[1] - t[0])
                    parts = (plus[0], plus[1], minus[0], minus[1])
                    turned = (minus[0], -minus[1], plus[0], -plus[1])
                    for i in range(4):
                        states[at_order, 4 * q + i] = parts[i]
                        states[orders + at_order, 4 * q + i] = turned[i]
                        states[2 * orders + at_order, 4 * q + i] = 0.5 * parts[i]
            return carry

        lax.fori_loop(0, n, unpack, 0)

        def one_order(t, carry):
            def add(a, total):
                b = partner[t * orders + a]
                vp, vm, yp, ym, wp, wm = (
                    (states[a, 2 * q], states[a, 2 * q + 1], states[b, 2 * q], states[b, 2 * q + 1])
                    for q in range(6)
                )

                def square(v):
                    ar, ai, br, bi = v
                    return ar * br - ai * bi, ar * bi + ai * br

                def cross(v, w):
                    ar, ai, br, bi = v
                    cr, ci, dr, di = w
                    return (
                        (ar * dr - ai * di) + (cr * br - ci * bi),
                        (ar * di + ai * dr) + (cr * bi + ci * br),
                    )

                terms = []
                for v, y in ((vp, yp), (vm, ym)):
                    first_term, second_term = square(v), square(y)
                    terms += [first_term[0] - second_term[0], first_term[1] - second_term[1]]
                heat, other = cross(ym, wp), cross(yp, wm)
                terms += [heat[0] + other[0], heat[1] + other[1]]
                bent, other = cross(ym, vp), cross(yp, vm)
                terms += [bent[0] - other[0], bent[1] - other[1]]
                return tuple(v + w for v, w in zip(total, terms))

            pr, pi, mr, mi, hr, hi, er, ei = lax.fori_loop(0, orders, add, (zero,) * 8, unroll=4)
            rows = [pi - mi, mr - pr, pr + mr, pi + mi, -hr, -hi, ei, -er]
            rows = (0.5 * jnp.concatenate(rows, axis=0)).astype(jnp.bfloat16)
            sums[c, t // 2, pl.ds(pl.multiple_of(lax.rem(t, 2) * 8 * radii, 8 * radii), 8 * radii), :] = rows
            return carry

        lax.fori_loop(0, orders, one_order, 0)
        for step in far_first(n):
            back_copy(target(*step), me, c).start()
        got[c, me] = sums[c, me]
        return carry

    lax.fori_loop(0, chunks, chunk_step, 0)
    loads[3].wait()

    contract = (((1,), (1,)), ((), ()))
    own_group = me // halves
    for k in group_order(n, groups):
        g = lax.rem(own_group // k[2] + k[0], groups // k[2]) * k[2] + lax.rem(
            lax.rem(own_group, k[2]) + k[1], k[2]
        )
        rows = pl.ds(pl.multiple_of(g * radii, radii), radii)
        total = jnp.zeros((16 * radii, slots), jnp.float32)
        for h in range(halves):
            source = halves * g + h

            @pl.when(source != me)
            def _(source=source):
                for c in range(chunks):
                    back_copy(source, source, c).wait_recv()

            total += lax.dot_general(
                jnp.concatenate([got[c, source] for c in range(chunks)], axis=1),
                analysis[:, h * width : (h + 1) * width],
                contract, preferred_element_type=jnp.float32,
            )
        total = total.reshape(2, 4, 2, radii, slots)
        added = jnp.where(first, total[0], jnp.where(second, total[1], 0.0))
        last, start = [], []
        for f in range(4):
            scale = inner[2 * f : 2 * f + 1]
            for c in range(2):
                b = right[f, c, rows, :] + added[f, c]
                ahead, back = b, b
                ratio = rho[2 * f : 2 * f + 1]
                step = 1
                while step < radii:
                    ahead += ratio * jnp.where(at >= step, pltpu.roll(ahead, step, 0), 0.0)
                    back += ratio * jnp.where(
                        at < radii - step, pltpu.roll(back, radii - step, 0), 0.0
                    )
                    ratio = ratio * ratio
                    step *= 2
                right[f, c, rows, :] = scale * (ahead + back - b)
                last.append(ahead[radii - 1 : radii])
                start.append(back[0:1])
        carries[g, 0] = jnp.concatenate(last, axis=0)
        carries[g, 1] = jnp.concatenate(start, axis=0)

    hop = power(float(radii))
    ahead_at, back_at = [], []
    total = jnp.zeros((8, slots), jnp.float32)
    for g in range(groups):
        ahead_at.append(total)
        total = hop * total + carries[g, 0]
    edges[row, 0:8] = total
    total = jnp.zeros((8, slots), jnp.float32)
    for g in reversed(range(groups)):
        back_at.insert(0, total)
        total = hop * total + carries[g, 1]
    edges[row, 8:16] = total

    def edge_copy(e, source):
        return pltpu.make_async_remote_copy(
            src_ref=edges.at[row], dst_ref=edges.at[source],
            send_sem=edge_send.at[e], recv_sem=edge_recv.at[source],
            device_id={"row": e}, device_id_type=pl.DeviceIdType.MESH,
        )

    for k in range(1, rows_count):
        edge_copy(lax.rem(row + k, rows_count), row).start()

    before = (row * points).astype(jnp.float32)
    after = ((rows_count - 1 - row) * points).astype(jnp.float32)
    span = power(float(all_points + 1))
    scale = 1.0 / (1.0 - span * span)
    to_start, to_end = power(before), power(after)
    rise = [jnp.exp(log_rho[2 * f : 2 * f + 1] * near) for f in range(4)]
    fall = [jnp.exp(log_rho[2 * f : 2 * f + 1] * far) for f in range(4)]
    shifts = [power(float(k * points)) for k in range(rows_count)]
    inside = [power(float(k * radii)) for k in range(groups)]

    for c in range(chunks):
        for k in range(1, n):
            e = lax.rem(me + k, n)
            grid_copy(e, e, c).wait_send()
            back_copy(e, e, c).wait_send()
    for k in range(1, rows_count):
        e = lax.rem(row + k, rows_count)
        edge_copy(e, e).wait()

    zero = jnp.zeros((8, slots), jnp.float32)
    ahead_in, back_in, ahead_all, back_all = zero, zero, zero, zero
    for e in range(rows_count):
        f_e, g_e = edges[e, 0:8], edges[e, 8:16]
        weight, reverse = zero, zero
        for k in range(rows_count - 1):
            weight = jnp.where(row - 1 - e == k, shifts[k], weight)
            reverse = jnp.where(e - row - 1 == k, shifts[k], reverse)
        ahead_in += weight * f_e
        back_in += reverse * g_e
        ahead_all += shifts[rows_count - 1 - e] * f_e
        back_all += shifts[e] * g_e
    low = inner * rho * back_all
    high = inner * rho * ahead_all
    left = inner * ahead_in + (span * high - low) * scale * to_start
    rest = inner * back_in + (span * low - high) * scale * to_end
    for g in range(groups):
        here = left * inside[g] + inner * ahead_at[g]
        there = rest * inside[groups - 1 - g] + inner * back_at[g]
        for f in range(4):
            for c in range(2):
                i = 2 * f + c
                value = right[f, c, g * radii : (g + 1) * radii, :]
                value = value + here[i : i + 1] * rise[f] + there[i : i + 1] * fall[f]
                out[f, c, g * radii : (g + 1) * radii, :] = jnp.where(held, value, 0.0)


def group_order(n, groups):
    inner = 2 if groups % 2 == 0 and n == 2 * groups else 1
    steps = [(dy, dx, inner) for dy in range(groups // inner) for dx in range(inner)]
    return sorted(steps, key=lambda d: (d[0] > 0) + d[1])


def triad_table(pair_index):
    orders = jnp.stack([pair_index, LMAX - pair_index], axis=1).reshape(-1)
    count = orders.shape[0]
    need = orders[:, None] - orders[None, :]
    match = jnp.abs(need)[:, :, None] == orders[None, None, :]
    at = jnp.arange(count, dtype=jnp.int32)
    place = jnp.min(jnp.where(match, at, 3 * count), axis=2)
    place = jnp.where(jnp.logical_and(need < 0, place < count), place + count, place)
    place = jnp.where(need == orders[None, :], at[None, :] + 2 * count, place)
    return jnp.where(need > orders[None, :], 3 * count, place).reshape(-1)


def local(n, rows_count, spectra, dtheta, dphi, analysis, pair_index, diffusivity):
    points, slots = spectra.shape[2], spectra.shape[3]
    radii = RADII
    halves = n * radii // points
    width = -(-dtheta.shape[1] // (128 * halves)) * 128
    extra = width * halves - dtheta.shape[1]
    if extra:
        dtheta, dphi, analysis = (jnp.pad(v, ((0, 0), (0, extra))) for v in (dtheta, dphi, analysis))
    chunks = width // 128
    vmem = pl.BlockSpec(memory_space=pltpu.VMEM)
    smem = pl.BlockSpec(memory_space=pltpu.SMEM)
    hbm = pl.BlockSpec(memory_space=pltpu.HBM)
    shape = spectra.shape
    table = pltpu.VMEM(dtheta.shape, jnp.bfloat16)
    return pl.pallas_call(
        functools.partial(step_kernel, n, rows_count),
        out_shape=jax.ShapeDtypeStruct(shape, jnp.float32),
        in_specs=[smem, smem, smem, hbm, hbm, hbm, hbm],
        out_specs=vmem,
        scratch_shapes=[
            pltpu.VMEM(shape, jnp.float32),
            table,
            table,
            table,
            pltpu.VMEM((chunks, n, 24 * radii, 128), jnp.bfloat16),
            pltpu.VMEM((chunks, n, 24 * radii, 128), jnp.bfloat16),
            pltpu.VMEM((6 * n + 1, 12, radii, 128), jnp.float32),
            pltpu.VMEM((chunks, n, 16 * radii, 128), jnp.bfloat16),
            pltpu.VMEM((chunks, n, 16 * radii, 128), jnp.bfloat16),
            pltpu.VMEM((rows_count, 16, slots), jnp.float32),
            pltpu.VMEM(shape, jnp.float32),
            pltpu.VMEM((points // radii, 2, 8, slots), jnp.float32),
            pltpu.SemaphoreType.DMA((4,)),
            pltpu.SemaphoreType.DMA((chunks, n)),
            pltpu.SemaphoreType.DMA((chunks, n)),
            pltpu.SemaphoreType.DMA((chunks, n)),
            pltpu.SemaphoreType.DMA((chunks, n)),
            pltpu.SemaphoreType.DMA((rows_count,)),
            pltpu.SemaphoreType.DMA((rows_count,)),
        ],
        compiler_params=pltpu.CompilerParams(
            collective_id=0, has_side_effects=True, vmem_limit_bytes=VMEM_LIMIT
        ),
        name="step",
    )(triad_table(pair_index), pair_index, diffusivity, spectra, dtheta, dphi, analysis)


def solution(mesh):
    n, rows_count = mesh.shape["ma"], mesh.shape["row"]
    return jax.shard_map(
        functools.partial(local, n, rows_count),
        mesh=mesh,
        in_specs=(
            P(None, None, "row", "ma"),
            P("ma", None),
            P("ma", None),
            P("ma", None),
            P(),
            P(),
        ),
        out_specs=P(None, None, "row", "ma"),
        check_vma=False,
    )
```
